128 devices in a mesh: ha: 8 (over x, y_lo), wa: 16 (over y_hi, z, core).
Axes of the slice: x: 4, y: 4 (y_hi: 2, y_lo: 2; y = y_hi * 2 + y_lo), z: 4, core: 2. Of those that a mesh axis runs over, the one named last changes fastest.
Arguments:
- latent: bfloat16 [16, 32, 128, 320], P(None, 'ha', 'wa'), may hold values from -40 to 40, as said below
- cotangent: bfloat16 [16, 32, 128, 320], P(None, 'ha', 'wa'), may hold values from -40 to 40, as said below
- w_fine: bfloat16 [9, 320, 320], replicated, may hold values from -0.109375 to 0.109375
- w_down: bfloat16 [4, 320, 640], replicated, may hold values from -0.15625 to 0.15625
- w_coarse: bfloat16 [9, 640, 640], replicated, may hold values from -0.078125 to 0.078125
- w_up: bfloat16 [4, 640, 320], replicated, may hold values from -0.25 to 0.25
Outputs:
- output: bfloat16 [16, 32, 128, 320], P(None, 'ha', 'wa')
- grad_latent: bfloat16 [16, 32, 128, 320], P(None, 'ha', 'wa')
- grad_fine: float32 [9, 320, 320], P(None, 'ha', 'wa')
- grad_down: float32 [4, 320, 640], P(None, 'ha', 'wa')
- grad_coarse: float32 [9, 640, 640], P(None, 'ha', 'wa')
- grad_up: float32 [4, 640, 320], P(None, 'ha', 'wa')
The draws below stay inside these ranges and needn't reach their ends.
Inputs may be any that keep to these rules, and one draw needn't show every extreme that they name: `latent`: finite activations of order one. `cotangent`: finite gradients.
All inputs are finite; a program needn't handle non-finite values.
Results may differ from the reference program's by a relative error of at most 0.014.
Values may be sent and summed in bfloat16 or wider, within the bound.
No kernel may reach another device: no remote copies, remote signals or barrier semaphores. Data moves between devices by JAX's collectives and lax.ppermute only.
A program may use at most 192 MiB of HBM per device.

```python
import math
import jax
import jax.numpy as jnp
from jax import lax

C1 = 320
C2 = 640
G = 32
F = 16
H = 32
W = 128


def draw_latent(key, part):
    key = jax.random.fold_in(key, 7)
    base_key, chan_key = jax.random.split(key)
    shape = (F, H, W, C1)
    rows_pos = jnp.arange(H, dtype=jnp.float32) / max(H - 1, 1)
    cols_pos = jnp.arange(W, dtype=jnp.float32) / max(W - 1, 1)
    ramp = jnp.exp(math.log(3.0) * 0.5 * (rows_pos[:, None] + cols_pos[None, :]))
    chan_scale = jnp.exp(jax.random.uniform(chan_key, (F, 1, 1, C1), jnp.float32, -0.7, 0.7))
    base = jnp.clip(jax.random.normal(base_key, shape, jnp.float32), -5.0, 5.0)
    return (base * ramp[None, :, :, None] * chan_scale).astype(jnp.bfloat16)


def draw_cotangent(key, part):
    key = jax.random.fold_in(key, 11)
    base_key, chan_key, frame_key = jax.random.split(key, 3)
    shape = (F, H, W, C1)
    rows_pos = jnp.arange(H, dtype=jnp.float32) / max(H - 1, 1)
    cols_pos = jnp.arange(W, dtype=jnp.float32) / max(W - 1, 1)
    chan_scale = jnp.exp(jax.random.uniform(chan_key, (F, 1, 1, C1), jnp.float32, -0.5, 0.5))
    ramp = jnp.exp(math.log(4.0) * 0.5 * (rows_pos[:, None] + cols_pos[None, :]))
    offset = jax.random.uniform(frame_key, (F, 1, 1, 1), jnp.float32, 0.4, 0.8)
    base = jnp.clip(jax.random.normal(base_key, shape, jnp.float32), -4.0, 4.0) + offset
    return (base * ramp[None, :, :, None] * chan_scale).astype(jnp.bfloat16)


def bell_draw(stream_key, shape, scale, bound, held_as=jnp.bfloat16):
    values = scale * jax.random.normal(stream_key, shape, jnp.float32)
    return jnp.clip(values, min=-bound, max=bound).astype(held_as)


def setup_inputs(seed: int = 0) -> dict:
    key_list = jax.random.split(jax.random.key(seed), 7)
    return {
        "latent": draw_latent(jax.random.fold_in(key_list[6], 71), 0),
        "cotangent": draw_cotangent(jax.random.fold_in(key_list[6], 71), 0),
        "w_fine": bell_draw(key_list[2], (9, C1, C1), (9 * C1) ** -0.5, 0.109375),
        "w_down": bell_draw(key_list[3], (4, C1, C2), (4 * C1) ** -0.5, 0.15625),
        "w_coarse": bell_draw(key_list[4], (9, C2, C2), (9 * C2) ** -0.5, 0.078125),
        "w_up": bell_draw(key_list[5], (4, C2, C1), C2 ** -0.5, 0.25),
    }


EPS = 1e-05

def silu_grad(value):
    sig = jax.nn.sigmoid(value)
    return sig * (1.0 + value * (1.0 - sig))

def pad_grid(value):
    return jnp.pad(value, ((0, 0), (1, 1), (1, 1), (0, 0)))

def conv_taps(padded, weight, rows, cols):
    frames, cin = (padded.shape[0], padded.shape[-1])
    total = None
    for tap in range(9):
        off_h, off_w = (tap // 3, tap % 3)
        piece = padded[:, off_h:off_h + rows, off_w:off_w + cols, :].reshape(-1, cin)
        term = jnp.dot(piece, weight[tap], preferred_element_type=jnp.float32)
        total = term if total is None else total + term
    return total.reshape(frames, rows, cols, weight.shape[2])

def conv_back(padded, weight, rows, cols):
    frames, cout = (padded.shape[0], padded.shape[-1])
    total = None
    for tap in range(9):
        off_h, off_w = (2 - tap // 3, 2 - tap % 3)
        piece = padded[:, off_h:off_h + rows, off_w:off_w + cols, :].reshape(-1, cout)
        term = lax.dot_general(piece, weight[tap], (((1,), (1,)), ((), ())), preferred_element_type=jnp.float32)
        total = term if total is None else total + term
    return total.reshape(frames, rows, cols, weight.shape[1])

def conv_weight(padded, grad, rows, cols):
    cin = padded.shape[-1]
    flat = grad.reshape(-1, grad.shape[-1])
    parts = []
    for tap in range(9):
        off_h, off_w = (tap // 3, tap % 3)
        piece = padded[:, off_h:off_h + rows, off_w:off_w + cols, :].reshape(-1, cin)
        parts.append(lax.dot_general(piece, flat, (((0,), (0,)), ((), ())), preferred_element_type=jnp.float32))
    return jnp.stack(parts)

def to_depth(value):
    frames, rows, cols, chan = value.shape
    value = value.reshape(frames, rows // 2, 2, cols // 2, 2, chan).transpose(0, 1, 3, 2, 4, 5)
    return value.reshape(frames * (rows // 2) * (cols // 2), 4 * chan)

def from_depth(value, frames, rows, cols, chan):
    value = value.reshape(frames, rows // 2, cols // 2, 2, 2, chan).transpose(0, 1, 3, 2, 4, 5)
    return value.reshape(frames, rows, cols, chan)

def reference(latent, cotangent, w_fine, w_down, w_coarse, w_up):
    frames, height, width, chan = latent.shape
    coarse_ch = w_coarse.shape[2]
    group_width = chan // G
    count = height * width * group_width
    latent_f = latent.astype(jnp.float32)
    grouped = latent_f.reshape(frames, height * width, G, group_width)
    mean = lax.optimization_barrier(jnp.sum(grouped, axis=(1, 3), keepdims=True)) / count
    meansq = lax.optimization_barrier(jnp.sum(grouped * grouped, axis=(1, 3), keepdims=True)) / count
    rstd = lax.rsqrt(meansq - mean * mean + EPS)
    normed = (grouped - mean) * rstd
    act = jax.nn.silu(normed).astype(jnp.bfloat16).reshape(frames, height, width, chan)
    act_pad = pad_grid(act)
    resid = (latent_f + conv_taps(act_pad, w_fine, height, width)).astype(jnp.bfloat16)
    depth = to_depth(resid)
    down_flat = w_down.reshape(4 * chan, coarse_ch)
    lowered = jnp.dot(depth, down_flat, preferred_element_type=jnp.float32).astype(jnp.bfloat16)
    lowered = lowered.reshape(frames, height // 2, width // 2, coarse_ch)
    lowered_f = lowered.astype(jnp.float32)
    coarse_act = jax.nn.silu(lowered_f).astype(jnp.bfloat16)
    coarse_pad = pad_grid(coarse_act)
    coarse = (lowered_f + conv_taps(coarse_pad, w_coarse, height // 2, width // 2)).astype(jnp.bfloat16)
    up_flat = jnp.transpose(w_up, (1, 0, 2)).reshape(coarse_ch, 4 * chan)
    coarse_flat = coarse.reshape(-1, coarse_ch)
    raised = jnp.dot(coarse_flat, up_flat, preferred_element_type=jnp.float32)
    output = (resid.astype(jnp.float32) + from_depth(raised, frames, height, width, chan)).astype(jnp.bfloat16)
    scale = float(frames * height * width) ** (-0.5)
    grad_depth = to_depth(cotangent)
    grad_up = lax.dot_general(coarse_flat, grad_depth, (((0,), (0,)), ((), ())), preferred_element_type=jnp.float32)
    grad_up = jnp.transpose(grad_up.reshape(coarse_ch, 4, chan), (1, 0, 2)) * scale
    gcoarse = lax.dot_general(grad_depth, up_flat, (((1,), (1,)), ((), ())), preferred_element_type=jnp.float32)
    gcoarse = gcoarse.astype(jnp.bfloat16).reshape(frames, height // 2, width // 2, coarse_ch)
    grad_coarse = conv_weight(coarse_pad, gcoarse, height // 2, width // 2) * scale
    back = conv_back(pad_grid(gcoarse), w_coarse, height // 2, width // 2)
    glow = (gcoarse.astype(jnp.float32) + back * silu_grad(lowered_f)).astype(jnp.bfloat16)
    glow_flat = glow.reshape(-1, coarse_ch)
    grad_down = lax.dot_general(depth, glow_flat, (((0,), (0,)), ((), ())), preferred_element_type=jnp.float32)
    grad_down = grad_down.reshape(4, chan, coarse_ch) * scale
    spread = lax.dot_general(glow_flat, down_flat, (((1,), (1,)), ((), ())), preferred_element_type=jnp.float32)
    gresid = (cotangent.astype(jnp.float32) + from_depth(spread, frames, height, width, chan)).astype(jnp.bfloat16)
    grad_fine = conv_weight(act_pad, gresid, height, width) * scale
    gact = conv_back(pad_grid(gresid), w_fine, height, width).reshape(frames, height * width, G, group_width)
    gnorm = gact * silu_grad(normed)
    first = lax.optimization_barrier(jnp.sum(gnorm, axis=(1, 3), keepdims=True)) / count
    second = lax.optimization_barrier(jnp.sum(gnorm * normed, axis=(1, 3), keepdims=True)) / count
    gx = rstd * (gnorm - first - normed * second)
    grad_latent = gresid.astype(jnp.float32).reshape(frames, height * width, G, group_width) + gx
    grad_latent = grad_latent.astype(jnp.bfloat16).reshape(frames, height, width, chan)
    return (output, grad_latent, grad_fine, grad_down, grad_coarse, grad_up)
```

```python
import functools

import jax
import jax.numpy as jnp
from jax import lax
from jax.experimental import pallas as pl
from jax.experimental.pallas import tpu as pltpu
from jax.sharding import PartitionSpec as P


BF = jnp.bfloat16
F32 = jnp.float32
EPS = 1e-05
C1, C2 = 320, 640
B = 64
COUNT = 32.0 * 128.0 * 10.0
VMEM = 32 * 1024 * 1024


def nn(a, b):
    return lax.dot_general(a, b, (((1,), (0,)), ((), ())), preferred_element_type=F32)


def nt(a, b):
    return lax.dot_general(a, b, (((1,), (1,)), ((), ())), preferred_element_type=F32)


def tn(a, b):
    return lax.dot_general(a, b, (((0,), (0,)), ((), ())), preferred_element_type=F32)


def iota(shape, dim):
    return lax.broadcasted_iota(jnp.int32, shape, dim)


def one_hot(cond):
    return jnp.where(cond, 1.0, 0.0).astype(BF)


def arrival_of(q):
    row, par, col = (q >> 7, (q >> 6) & 1, q & 63)
    return ((col >> 2) << 5) + (row << 3) + ((col & 3) << 1) + par


def to_parity(which):
    q, a = (iota((512, 1024), 0), iota((512, 1024), 1))
    return one_hot((arrival_of(q) == ((a >> 6) << 5) + (a & 31)) & (((a >> 5) & 1) == which))


def from_parity():
    return one_hot(arrival_of(iota((512, 512), 1)) == iota((512, 512), 0))


def prev_col(v):
    return jnp.where(iota(v.shape, 0) == 0, 0.0, pltpu.roll(v, 1, 0))


def next_col(v):
    return jnp.where(iota(v.shape, 0) == B - 1, 0.0, pltpu.roll(v, B - 1, 0))


def group_sums(sums):
    same = ((iota((C1, C1), 0) * 6554) >> 16) == ((iota((C1, C1), 1) * 6554) >> 16)
    return lax.dot_general(
        sums,
        jnp.where(same, 1.0, 0.0).astype(F32),
        (((1,), (0,)), ((), ())),
        precision=lax.Precision.HIGHEST,
        preferred_element_type=F32,
    )


def group_sums(sums):
    same = ((iota((C1, C1), 0) * 6554) >> 16) == ((iota((C1, C1), 1) * 6554) >> 16)
    return lax.dot_general(
        sums,
        jnp.where(same, 1.0, 0.0).astype(F32),
        (((1,), (0,)), ((), ())),
        precision=lax.Precision.HIGHEST,
        preferred_element_type=F32,
    )


def norm_of(st_ref):
    totals = group_sums(st_ref[...]) / COUNT
    mean = totals[0:1]
    return mean, lax.rsqrt(totals[1:2] - mean * mean + EPS)


def sigmoid(v):
    return 1.0 / (1.0 + jnp.exp(-v))


def silu_grad(v):
    s = sigmoid(v)
    return s * (1.0 + v * (1.0 - s))


def rows8(a, b):
    return jnp.concatenate([a, b, jnp.zeros((6, a.shape[1]), F32)], axis=0)


def call(kernel, outs, n_in, scratch=(), smem=0, hbm=0, us=2, after=()):
    first = smem + n_in + hbm

    def body(*refs):
        kernel(*refs[:first], *refs[first + len(after) :])

    f = pl.pallas_call(
        body,
        out_shape=outs,
        in_specs=[pl.BlockSpec(memory_space=pltpu.SMEM)] * smem
        + [pl.BlockSpec(memory_space=pltpu.VMEM)] * n_in
        + [pl.BlockSpec(memory_space=pl.ANY)] * (hbm + len(after)),
        out_specs=jax.tree.map(lambda _: pl.BlockSpec(memory_space=pltpu.VMEM), outs),
        scratch_shapes=list(scratch),
        compiler_params=pltpu.CompilerParams(vmem_limit_bytes=VMEM),
        cost_estimate=pl.CostEstimate(flops=us * 10**9, bytes_accessed=10**6, transcendentals=0),
    )
    return lambda *args: f(*args, *after)


def sds(shape, dtype=BF):
    return jax.ShapeDtypeStruct(shape, dtype)


def turn_kernel(count, *refs):
    for src, dst in zip(refs[:count], refs[-count:]):
        dst[0] = jnp.transpose(src[0])


def turned(weights, us, after=()):
    def spec(rows, cols):
        return pl.BlockSpec((1, rows, cols), lambda t: (t, 0, 0))

    outs = [(w.shape[0], w.shape[2], w.shape[1]) for w in weights]
    return pl.pallas_call(
        functools.partial(turn_kernel, len(weights)),
        grid=(weights[0].shape[0],),
        out_shape=[sds(o) for o in outs],
        in_specs=[spec(*w.shape[1:]) for w in weights] + [pl.BlockSpec(memory_space=pl.ANY)] * len(after),
        out_specs=[spec(*o[1:]) for o in outs],
        compiler_params=pltpu.CompilerParams(vmem_limit_bytes=VMEM),
        cost_estimate=pl.CostEstimate(flops=us * 10**9, bytes_accessed=10**6, transcendentals=0),
    )(*weights, *after)


def sort_kernel(a_ref, wu, x_ref, up_ref, down_ref, c_ref, cot_ref, g_ref, st_ref):
    x = nn(to_parity(0), a_ref[...])
    c = nn(to_parity(1), a_ref[...]).astype(BF)
    xb = x.astype(BF)
    x_ref[...] = xb
    c_ref[...] = c
    for k in range(4):
        for h in range(2):
            at = (2 * h + k // 2) * 128 + (k % 2) * B
            cot_ref[h * B : h * B + B, k * C1 : (k + 1) * C1] = c[at : at + B]
    g = nn(cot_ref[...], wu[...]).astype(BF)
    g_ref[...] = g
    up_ref[0:384, :] = xb[0:384]
    up_ref[384:448, :] = g[0:B, 0:C1]
    up_ref[448:512, :] = g[0:B, C1:C2]
    down_ref[0:384, :] = xb[128:512]
    down_ref[384:448, :] = g[B : 2 * B, 0:C1]
    down_ref[448:512, :] = g[B : 2 * B, C1:C2]
    st_ref[...] = rows8(jnp.sum(x, axis=0, keepdims=True), jnp.sum(x * x, axis=0, keepdims=True))


def fetch(pairs, sems):
    copies = [pltpu.make_async_copy(src, dst, sems.at[n]) for n, (src, dst) in enumerate(pairs)]
    for c in copies:
        c.start()
    return copies


def forward_kernel(
    edge, x_ref, xd_ref, xu_ref, st_ref, wf_h, wd_h, wc_h, wu_h,
    send_ref, ave_ref, avo_ref, low_ref, cact_ref, coarse_ref, depth_ref,
    ve, vo, d, cv, ox, wf, wd, wc, wu, sems,
):
    copies = fetch([(wf_h, wf), (wd_h, wd), (wc_h, wc), (wu_h, wu)], sems)
    mean, rstd = norm_of(st_ref)
    in_top = jnp.where(edge[0] == 1, 0.0, 1.0)
    in_bot = jnp.where(edge[1] == 1, 0.0, 1.0)

    def latent(row, par):
        ref, base = (xd_ref, row + 3) if row < 0 else (x_ref, row) if row < 4 else (xu_ref, row - 4)
        return ref[base * 128 + par * B : base * 128 + par * B + B, :].astype(F32)

    for row in range(-3, 7):
        at = slice((row + 3) * B, (row + 4) * B)
        for par in range(2):
            z = (latent(row, par) - mean) * rstd
            act = z * sigmoid(z)
            if row < 0:
                act = act * in_top
            if row > 3:
                act = act * in_bot
            ab = act.astype(BF)
            if par == 0:
                ve[at, C1 : 2 * C1] = ab
                vo[at, 0:C1] = ab
                vo[at, 2 * C1 : 3 * C1] = next_col(act).astype(BF)
            else:
                ve[at, 2 * C1 : 3 * C1] = ab
                vo[at, C1 : 2 * C1] = ab
                ve[at, 0:C1] = prev_col(act).astype(BF)

    ave_ref[...] = ve[2 * B : 8 * B, :]
    avo_ref[...] = vo[2 * B : 8 * B, :]
    copies[0].wait()
    for par, v in ((0, ve), (1, vo)):
        acc = nn(v[0:512, :], wf[0]) + nn(v[B : B + 512, :], wf[1]) + nn(v[2 * B : 2 * B + 512, :], wf[2])
        for rr in range(8):
            k = 2 * (rr % 2) + par
            r = latent(rr - 2, par) + acc[rr * B : rr * B + B]
            d[(rr // 2) * B : (rr // 2) * B + B, k * C1 : (k + 1) * C1] = r.astype(BF)
    depth_ref[...] = d[B : 3 * B, :]

    copies[1].wait()
    low = nn(d[...], wd[...]).astype(BF)
    low_ref[...] = low[B : 3 * B]
    for h in range(4):
        lf = low[h * B : h * B + B].astype(F32)
        ca = lf * sigmoid(lf)
        if h == 0:
            ca = ca * in_top
        if h == 3:
            ca = ca * in_bot
        s = slice(h * B, h * B + B)
        cv[s, 0:C2] = prev_col(ca).astype(BF)
        cv[s, C2 : 2 * C2] = ca.astype(BF)
        cv[s, 2 * C2 : 3 * C2] = next_col(ca).astype(BF)
    cact_ref[...] = cv[B : 3 * B, C2 : 2 * C2]
    copies[2].wait()
    acc = low[B : 3 * B].astype(F32)
    for i in range(3):
        acc = acc + nn(cv[i * B : i * B + 128, :], wc[i])
    coarse = acc.astype(BF)
    coarse_ref[...] = coarse
    copies[3].wait()
    for k in range(4):
        up = nn(coarse, wu[k])
        for h in range(2):
            at = (2 * h + k // 2) * 128 + (k % 2) * B
            o = d[(h + 1) * B : (h + 2) * B, k * C1 : (k + 1) * C1].astype(F32) + up[h * B : h * B + B]
            ox[at : at + B, :] = o.astype(BF)
    send_ref[...] = nn(from_parity(), ox[...]).astype(BF)


def gcoarse_kernel(me, g_ref, hd_ref, hu_ref, cact_ref, wc_h, m0, m1, m2, m3, back_ref, gv, wc, sems):
    copies = fetch([(wc_h.at[i], wc.at[i]) for i in (2, 1, 0)], sems)
    gv[B : 3 * B, C2 : 2 * C2] = g_ref[...]
    for s, ref in ((slice(0, B), hd_ref), (slice(3 * B, 4 * B), hu_ref)):
        gv[s, C2 : C2 + C1] = ref[384:448, :]
        gv[s, C2 + C1 : 2 * C2] = ref[448:512, :]
    for h in range(4):
        s = slice(h * B, h * B + B)
        gf = gv[s, C2 : 2 * C2].astype(F32)
        gv[s, 0:C2] = next_col(gf).astype(BF)
        gv[s, 2 * C2 : 3 * C2] = prev_col(gf).astype(BF)
    q = iota((C2, 160), 1)
    core = jnp.where(q >= 80, 1, 0)
    hi = jnp.where(q - 80 * core >= 40, 1, 0)
    channel = (hi * 8 + core) * 40 + q - 80 * core - 40 * hi
    for n, ref in enumerate((m0, m1, m2, m3)):
        pick = one_hot(iota((C2, 160), 0) == channel + lax.rem(me[3] + n, 4) * 80)
        part = nn(gv[:, C2 : 2 * C2], pick).astype(BF)
        ref[:, 0:C2] = cact_ref[...]
        ref[:, C2 : C2 + 160] = part[0:128]
        ref[:, C2 + 160 : C2 + 320] = part[128:256]
    back = None
    for n, i in enumerate((2, 1, 0)):
        copies[n].wait()
        t = nn(gv[(2 - i) * B : (2 - i) * B + 128, :], wc[i])
        back = t if back is None else back + t
    back_ref[...] = back


def gresid_kernel(c_ref, g_ref, back_ref, low_ref, wd, gres_ref, geo_ref, glow_ref, up_ref, down_ref):
    glow = g_ref[...].astype(F32) + back_ref[...] * silu_grad(low_ref[...].astype(F32))
    glow = glow.astype(BF)
    glow_ref[...] = glow
    for k in range(4):
        spread = nn(glow, wd[k])
        par = k % 2
        for h in range(2):
            row = 2 * h + k // 2
            s = slice(row * 128 + par * B, row * 128 + par * B + B)
            grb = (c_ref[s, :].astype(F32) + spread[h * B : h * B + B]).astype(BF)
            gres_ref[s, :] = grb
            geo_ref[par * 256 + row * B : par * 256 + row * B + B, :] = grb
            if row == 0:
                up_ref[par * B : par * B + B, :] = grb
            if row == 3:
                down_ref[par * B : par * B + B, :] = grb


def gnorm_kernel(x_ref, st_ref, geo, hd_ref, hu_ref, wf, gn_ref, st2_ref, rv):
    for row in range(-1, 5):
        to = slice((row + 1) * B, (row + 2) * B)
        for par in range(2):
            ref, at = (hd_ref, 0) if row < 0 else (hu_ref, 0) if row > 3 else (geo, row * B)
            at += par * (256 if 0 <= row < 4 else B)
            grb = ref[at : at + B, :]
            gr = grb.astype(F32)
            rv[1 + par, to, :] = grb
            if par == 0:
                rv[3, to, :] = next_col(gr).astype(BF)
            else:
                rv[0, to, :] = prev_col(gr).astype(BF)
    mean, rstd = norm_of(st_ref)
    s1 = jnp.zeros((1, C1), F32)
    s2 = jnp.zeros((1, C1), F32)
    for par in range(2):
        acc = None
        for i in range(3):
            for j in range(3):
                t = nt(rv[par + 2 - j, (2 - i) * B : (2 - i) * B + 256, :], wf[3 * i + j])
                acc = t if acc is None else acc + t
        for row in range(4):
            s = slice(row * 128 + par * B, row * 128 + par * B + B)
            z = (x_ref[s, :].astype(F32) - mean) * rstd
            gn = acc[row * B : row * B + B] * silu_grad(z)
            gn_ref[s, :] = gn
            s1 = s1 + jnp.sum(gn, axis=0, keepdims=True)
            s2 = s2 + jnp.sum(gn * z, axis=0, keepdims=True)
    st2_ref[...] = rows8(s1, s2)


def grad_latent_kernel(x_ref, st_ref, gn_ref, gres_ref, st2_ref, send_ref, out_ref):
    mean, rstd = norm_of(st_ref)
    m = group_sums(st2_ref[...]) / COUNT
    z = (x_ref[...].astype(F32) - mean) * rstd
    g = gres_ref[...].astype(F32) + rstd * (gn_ref[...] - m[0:1] - z * m[1:2])
    g = nn(from_parity(), g.astype(BF)).astype(BF)
    for f in range(16):
        out_ref[f, 0:32, :] = send_ref[32 * f : 32 * f + 32, :]
        out_ref[f, 32:64, :] = g[32 * f : 32 * f + 32]


def places(me, rows):
    q = iota((C2, rows), 0)
    core = jnp.where(q >= C1, 1, 0)
    rest = q - C1 * core
    block = (rest * 1639) >> 16
    return ((block & 1) ^ me[5]) * 8 + (block >> 1) * 2 + core, rest - 40 * block


def turn_grads_kernel(me, geo, cot, glow, gt, ct, lt):
    c = iota((C2, C1), 1)
    block, rest = places(me, C1)
    fine = one_hot((rest < 20) & (c == block * 20 + rest))
    up = one_hot((rest >= 20) & (c == block * 20 + rest - 20))
    gt[...] = nt(fine, geo[...]).astype(BF)
    for k in range(4):
        ct[k] = nt(up, cot[:, k * C1 : (k + 1) * C1]).astype(BF)
    block, rest = places(me, C2)
    lt[...] = nt(one_hot(iota((C2, C2), 1) == block * 40 + rest), glow[...]).astype(BF)


def weight_kernel(me, gt, ct, lt, ave, avo, coarse, depth, keep, send, acc):
    for slot, ref in ((0, keep), (1, send)):
        rows = pl.ds(pl.multiple_of((me[2] ^ slot) * C1, 64), C1)
        for i in range(3):
            s = slice(i * B, i * B + 256)
            both = jnp.concatenate([ave[s, :], avo[s, :]], axis=0)
            acc[:, i * 960 : (i + 1) * 960] = nn(gt[rows, :], both)
        for k in range(4):
            s = slice(k * C2, (k + 1) * C2)
            ref[:, s] = (acc[:, s] + nn(ct[k, rows, :], coarse[...])).astype(BF)
        ref[:, 2560:2880] = acc[:, 2560:2880].astype(BF)
        ref[:, 2880:2944] = jnp.zeros((C1, 64), BF)
        ref[:, 2944:4224] = nn(lt[rows, :], depth[...]).astype(BF)


def coarse_kernel(me, m0, m1, m2, m3, keep, send, a, res):
    eye = one_hot(iota((160, 160), 0) == iota((160, 160), 1))
    lane = iota((160, 256), 1) & 63
    for s, ref in enumerate((m0, m1, m2, m3)):
        f = nt(eye, jnp.concatenate([ref[:, C2 : C2 + 160], ref[:, C2 + 160 : C2 + 320]], axis=0))
        taps = (
            jnp.where(lane == 63, 0.0, pltpu.roll(f, 255, 1)),
            f,
            jnp.where(lane == 0, 0.0, pltpu.roll(f, 1, 1)),
        )
        at = slice(s * 128, s * 128 + 128)
        for j, v in enumerate(taps):
            mid = pltpu.roll(v, 192, 1)
            a[j * 160 : j * 160 + 160, at] = v[:, 128:256].astype(BF)
            a[(3 + j) * 160 : (3 + j) * 160 + 160, at] = mid[:, 0:128].astype(BF)
            a[(6 + j) * 160 : (6 + j) * 160 + 160, at] = v[:, 0:128].astype(BF)
    act = jnp.concatenate([m0[:, 0:C2], m1[:, 0:C2], m2[:, 0:C2], m3[:, 0:C2]], axis=0)
    res[...] = nn(a[...], act)
    for slot, ref in ((0, keep), (1, send)):
        for t in range(9):
            for e in range(2):
                at = t * 160 + (me[2] ^ slot) * 80 + (me[5] ^ e) * 40
                v = res[pl.ds(pl.multiple_of(at, 8), 40), :].astype(BF)
                for i in range(8):
                    to = lax.rem(i // 2 + 4 - me[0], 4) * 4 + ((i % 2) ^ me[1]) * 2 + e
                    ref[to, :, t * 80 : t * 80 + 80] = v[:, i * 80 : i * 80 + 80]


def pack_kernel(me, a_ref, o0, o1, o2, o3, acc, low, high, out):
    acc[...] = (a_ref[0].astype(F32) + a_ref[1].astype(F32)) + (a_ref[2].astype(F32) + a_ref[3].astype(F32))
    low[...] = jnp.zeros(low.shape, F32)
    high[...] = jnp.zeros(high.shape, F32)
    row = iota((80, 384), 0)
    first = jnp.where(row >= 40, row - 40, row) < 20
    for i in range(8):
        for t in range(9):
            low[:, t * 40 : t * 40 + 40] = acc[:, t * C1 + i * 40 : t * C1 + i * 40 + 40]
        for k in range(4):
            high[:, k * 80 : k * 80 + 80] = acc[:, k * C2 + i * 80 : k * C2 + i * 80 + 80]
        to = lax.rem(i // 2 + 4 - me[0], 4) * 2 + ((i % 2) ^ me[1])
        out[to, :, 0:384] = jnp.where(first, low[:, 0:384], high[:, 0:384]).astype(BF)
        for k in range(4):
            at = 2944 + k * C1 + i * 40
            high[:, 384 + k * 40 : 424 + k * 40] = acc[:, at : at + 40]
        out[to, :, 384:640] = high[:, 384:640].astype(BF)
    for n, ref in enumerate((o0, o1, o2, o3)):
        ref[...] = out[2 * n : 2 * n + 2]


def finish_kernel(scale, a_ref, b_ref, c_ref, d_ref, fine_ref, down_ref, coarse_ref, up_ref, u):
    total = a_ref[...].astype(F32) + b_ref[...].astype(F32)
    total = (total + c_ref[...].astype(F32) + d_ref[...].astype(F32)) * scale
    for t in range(9):
        fine_ref[t] = total[0:20, t * 40 : t * 40 + 40]
    u[...] = jnp.zeros(u.shape, F32)
    for k in range(4):
        up_ref[:, k, :] = total[20:40, k * 80 : k * 80 + 80]
        u[0:40, 0:40] = total[:, 384 + k * 40 : 424 + k * 40]
        down_ref[k] = jnp.transpose(u[...])[0:40, 0:40]
    for t in range(9):
        coarse_ref[t] = total[:, C2 + t * 80 : C2 + t * 80 + 80]


def pair_kernel(mine, got, *outs):
    for n, ref in enumerate(outs):
        s = slice(4 * n, 4 * n + 4)
        ref[...] = (mine[s].astype(F32) + got[s].astype(F32)).astype(BF)


def slab_kernel(mine, got, st, out_ref, st_ref):
    st_ref[...] = st[...]
    for n in range(8):
        out_ref[n] = (mine[n].astype(F32) + got[n].astype(F32)).astype(BF)


def add(*terms):
    total = terms[0].astype(F32)
    for t in terms[1:]:
        total = total + t.astype(F32)
    return total.astype(BF)


def other_core(v):
    return lax.ppermute(v, "wa", [(w, w ^ 1) for w in range(16)])


def ring_x(v, step):
    return lax.ppermute(v, "ha", [(h, ((h // 2 + step) % 4) * 2 + h % 2) for h in range(8)])


def other_y(v):
    return lax.ppermute(v, "ha", [(h, h ^ 1) for h in range(8)])


def ring_z(v, step):
    return lax.ppermute(
        v, "wa", [(w, (w // 8) * 8 + ((w // 2 + step) % 4) * 2 + w % 2) for w in range(16)]
    )


def other_y_hi(v):
    return lax.ppermute(v, "wa", [(w, w ^ 8) for w in range(16)])


def to_next(v):
    return lax.ppermute(v, "ha", [(h, h + 1) for h in range(7)])


def to_prev(v):
    return lax.ppermute(v, "ha", [(h + 1, h) for h in range(7)])


def swap_wa(v):
    return lax.all_to_all(v, "wa", 0, 0, tiled=True)


def other_both(v):
    pairs = [(h * 16 + w, (h ^ 1) * 16 + (w ^ 8)) for h in range(8) for w in range(16)]
    return lax.ppermute(v, ("ha", "wa"), pairs)


def swap_z(v):
    groups = [[hi * 8 + z * 2 + core for z in range(4)] for hi in range(2) for core in range(2)]
    return lax.all_to_all(v, "wa", 0, 0, axis_index_groups=groups, tiled=True)


def shards(latent, cotangent, w_fine, w_down, w_coarse, w_up):
    ha, wa = (lax.axis_index("ha"), lax.axis_index("wa"))
    edge = jnp.stack([ha == 0, ha == 7]).astype(jnp.int32)
    me = jnp.stack([ha // 2, ha % 2, wa % 2, (wa // 2) % 4, wa, wa // 8]).astype(jnp.int32)
    frames, rows, cols, _ = latent.shape
    scale = float(frames * 32 * 128) ** (-0.5)
    up_t = jnp.swapaxes(w_up, 1, 2)

    lat = latent.reshape(16, 32, C1)
    both = swap_wa(jnp.concatenate([lat, cotangent.reshape(16, 32, C1)], axis=1))
    (wct,) = turned([w_coarse], 9)
    x, up, down, c, cotk, g, st = call(
        sort_kernel,
        [
            sds((512, C1)),
            sds((512, C1)),
            sds((512, C1)),
            sds((512, C1)),
            sds((128, 4 * C1)),
            sds((128, C2)),
            sds((8, C1), F32),
        ],
        2,
        us=4,
        after=(wct,),
    )(both.reshape(1024, C1), up_t.reshape(4 * C1, C2))
    st_y = st + other_y(st)
    st = st_y + ring_x(st_y, 1) + ring_x(st_y, 2) + ring_x(st_y, 3)
    hd, hu = (to_next(down), to_prev(up))

    wdt, wun = turned([w_down, up_t], 4, after=(st_y,))
    dma = pltpu.SemaphoreType.DMA
    send, ave, avo, low, cact, coarse, depth = call(
        forward_kernel,
        [sds((512, C1)), sds((384, 3 * C1)), sds((384, 3 * C1)), sds((128, C2))]
        + [sds((128, C2)), sds((128, C2)), sds((128, 4 * C1))],
        4,
        [
            pltpu.VMEM((640, 3 * C1), BF),
            pltpu.VMEM((640, 3 * C1), BF),
            pltpu.VMEM((256, 4 * C1), BF),
            pltpu.VMEM((256, 3 * C2), BF),
            pltpu.VMEM((512, C1), BF),
            pltpu.VMEM((3, 3 * C1, C1), BF),
            pltpu.VMEM((4 * C1, C2), BF),
            pltpu.VMEM((3, 3 * C2, C2), BF),
            pltpu.VMEM((4, C2, C1), BF),
            dma((4,)),
        ],
        smem=1,
        hbm=4,
        us=11,
    )(
        edge, x, hd, hu, st,
        w_fine.reshape(3, 3 * C1, C1), w_down.reshape(4 * C1, C2), w_coarse.reshape(3, 3 * C2, C2), wun,
    )

    m0, m1, m2, m3, back = call(
        gcoarse_kernel,
        [sds((128, 960))] * 4 + [sds((128, C2), F32)],
        4,
        [pltpu.VMEM((256, 3 * C2), BF), pltpu.VMEM((3, 3 * C2, C2), BF), dma((3,))],
        smem=1,
        hbm=1,
        us=6,
    )(me, g, hd, hu, cact, wct.reshape(3, 3 * C2, C2))
    m1, m2, m3 = (ring_z(v, n + 1) for n, v in enumerate((m1, m2, m3)))

    gres, geo, glow, up, down = call(
        gresid_kernel,
        [sds((512, C1)), sds((512, C1)), sds((128, C2)), sds((128, C1)), sds((128, C1))],
        5,
        us=3,
    )(c, g, back, low, wdt)
    ed, eu = (to_next(down), to_prev(up))

    gt, ct, lt = call(
        turn_grads_kernel,
        [sds((C2, 512)), sds((4, C2, 128)), sds((C2, 128))],
        3,
        smem=1,
        us=3,
        after=(m1, m2, m3),
    )(me, geo, cotk, glow)
    kw, sw = call(
        weight_kernel,
        [sds((C1, 4224))] * 2,
        7,
        [pltpu.VMEM((C1, 2880), F32)],
        smem=1,
        us=7,
        after=(ed, eu),
    )(me, gt, ct, lt, ave, avo, coarse, depth)
    got_w = other_core(sw)
    gn, st2 = call(
        gnorm_kernel,
        [sds((512, C1), F32), sds((8, C1), F32)],
        6,
        [pltpu.VMEM((4, 384, C1), BF)],
        us=6,
        after=(sw,),
    )(x, st, geo, ed, eu, w_fine)
    pair_w, st2 = call(slab_kernel, [sds((8, 40, 4224)), sds((8, C1), F32)], 3, us=4)(
        kw.reshape(8, 40, 4224), got_w.reshape(8, 40, 4224), st2
    )
    sums_w = swap_z(pair_w.reshape(4, 80, 4224))
    st2_y = st2 + other_y(st2)
    st2 = st2_y + ring_x(st2_y, 1) + ring_x(st2_y, 2) + ring_x(st2_y, 3)
    kc, sc = call(
        coarse_kernel,
        [sds((16, 40, 720))] * 2,
        4,
        [pltpu.VMEM((1440, 512), BF), pltpu.VMEM((1440, C2), F32)],
        smem=1,
        us=1,
        after=(st2_y,),
    )(me, m0, m1, m2, m3)
    got_c = other_core(sc)

    pair_c = call(pair_kernel, [sds((4, 40, 720))] * 4, 2, us=1, after=(pair_w,))(kc, got_c)
    coarse_x = add(pair_c[0], *[ring_x(pair_c[n], n) for n in range(1, 4)])

    gsend = call(grad_latent_kernel, sds((16, 64, C1)), 6, us=1, after=(pair_c[0],))(
        x, st, gn, gres, st2, send
    )
    home = swap_wa(gsend)
    output = home[:, :32].reshape(frames, rows, cols, C1)
    grad_latent = home[:, 32:].reshape(frames, rows, cols, C1)

    packed = call(
        pack_kernel,
        [sds((2, 80, C2))] * 4,
        1,
        [
            pltpu.VMEM((80, 4224), F32),
            pltpu.VMEM((80, C2), F32),
            pltpu.VMEM((80, C2), F32),
            pltpu.VMEM((8, 80, C2), BF),
        ],
        smem=1,
        us=4,
        after=(coarse_x, gsend),
    )(me, sums_w)
    packed = add(packed[0], *[ring_x(packed[n], n) for n in range(1, 4)])
    joined = jnp.concatenate([packed.reshape(4, 40, C2), coarse_x], axis=2)
    fine, down, coarse_w, up = call(
        functools.partial(finish_kernel, scale),
        [sds((9, 20, 40), F32), sds((4, 40, 40), F32), sds((9, 40, 80), F32), sds((20, 4, 80), F32)],
        4,
        [pltpu.VMEM((128, 128), F32)],
    )(joined[0], other_y(joined[2]), other_y_hi(joined[1]), other_both(joined[3]))
    fine, coarse_w = (jnp.swapaxes(v, 1, 2) for v in (fine, coarse_w))
    return output, grad_latent, fine, down, coarse_w, jnp.transpose(up, (1, 2, 0))


def solution(mesh):
    big, small = (P(None, "ha", "wa", None), P(None, "ha", "wa"))
    return jax.shard_map(
        shards,
        mesh=mesh,
        in_specs=(big, big, P(), P(), P(), P()),
        out_specs=(big, big, small, small, small, small),
        check_vma=False,
    )
```

```python
import functools

import jax
import jax.numpy as jnp
from jax import lax
from jax.experimental import pallas as pl
from jax.experimental.pallas import tpu as pltpu
from jax.sharding import PartitionSpec as P


BF = jnp.bfloat16
F32 = jnp.float32
EPS = 1e-05
C1, C2 = 320, 640
B = 64
COUNT = 32.0 * 128.0 * 10.0
VMEM = 16 * 1024 * 1024


def nn(a, b):
    return lax.dot_general(a, b, (((1,), (0,)), ((), ())), preferred_element_type=F32)


def nt(a, b):
    return lax.dot_general(a, b, (((1,), (1,)), ((), ())), preferred_element_type=F32)


def tn(a, b):
    return lax.dot_general(a, b, (((0,), (0,)), ((), ())), preferred_element_type=F32)


def iota(shape, dim):
    return lax.broadcasted_iota(jnp.int32, shape, dim)


def one_hot(cond):
    return jnp.where(cond, 1.0, 0.0).astype(BF)


def arrival_of(q):
    row, par, col = (q >> 7, (q >> 6) & 1, q & 63)
    return ((col >> 2) << 5) + (row << 3) + ((col & 3) << 1) + par


def to_parity(which):
    q, a = (iota((512, 1024), 0), iota((512, 1024), 1))
    return one_hot((arrival_of(q) == ((a >> 6) << 5) + (a & 31)) & (((a >> 5) & 1) == which))


def from_parity():
    return one_hot(arrival_of(iota((512, 512), 1)) == iota((512, 512), 0))


def prev_col(v):
    return jnp.where(iota(v.shape, 0) == 0, 0.0, pltpu.roll(v, 1, 0))


def next_col(v):
    return jnp.where(iota(v.shape, 0) == B - 1, 0.0, pltpu.roll(v, B - 1, 0))


def group_sums(sums):
    same = ((iota((C1, C1), 0) * 6554) >> 16) == ((iota((C1, C1), 1) * 6554) >> 16)
    return lax.dot_general(
        sums,
        jnp.where(same, 1.0, 0.0).astype(F32),
        (((1,), (0,)), ((), ())),
        precision=lax.Precision.HIGHEST,
        preferred_element_type=F32,
    )


def group_sums(sums):
    same = ((iota((C1, C1), 0) * 6554) >> 16) == ((iota((C1, C1), 1) * 6554) >> 16)
    return lax.dot_general(
        sums,
        jnp.where(same, 1.0, 0.0).astype(F32),
        (((1,), (0,)), ((), ())),
        precision=lax.Precision.HIGHEST,
        preferred_element_type=F32,
    )


def norm_of(st_ref):
    totals = group_sums(st_ref[...]) / COUNT
    mean = totals[0:1]
    return mean, lax.rsqrt(totals[1:2] - mean * mean + EPS)


def sigmoid(v):
    return 1.0 / (1.0 + jnp.exp(-v))


def silu_grad(v):
    s = sigmoid(v)
    return s * (1.0 + v * (1.0 - s))


def rows8(a, b):
    return jnp.concatenate([a, b, jnp.zeros((6, a.shape[1]), F32)], axis=0)


def call(kernel, outs, n_in, scratch=(), smem=0, us=2, after=(), vmem=VMEM):
    first = smem + n_in

    def body(*refs):
        kernel(*refs[:first], *refs[first + len(after) :])

    f = pl.pallas_call(
        body,
        out_shape=outs,
        in_specs=[pl.BlockSpec(memory_space=pltpu.SMEM)] * smem
        + [pl.BlockSpec(memory_space=pltpu.VMEM)] * n_in
        + [pl.BlockSpec(memory_space=pl.ANY)] * len(after),
        out_specs=jax.tree.map(lambda _: pl.BlockSpec(memory_space=pltpu.VMEM), outs),
        scratch_shapes=list(scratch),
        compiler_params=pltpu.CompilerParams(vmem_limit_bytes=vmem),
        cost_estimate=pl.CostEstimate(flops=us * 10**9, bytes_accessed=10**6, transcendentals=0),
    )
    return lambda *args: f(*args, *after)


def sds(shape, dtype=BF):
    return jax.ShapeDtypeStruct(shape, dtype)


def turn_kernel(count, *refs):
    for src, dst in zip(refs[:count], refs[-count - 1 : -1]):
        dst[0] = jnp.transpose(src[0])
    refs[-1][...] = jnp.zeros((8, 128), F32)


def turned(weights, us, after=()):
    def spec(rows, cols):
        return pl.BlockSpec((1, rows, cols), lambda t: (t, 0, 0))

    outs = [(w.shape[0], w.shape[2], w.shape[1]) for w in weights]
    return pl.pallas_call(
        functools.partial(turn_kernel, len(weights)),
        grid=(weights[0].shape[0],),
        out_shape=[sds(o) for o in outs] + [sds((8, 128), F32)],
        in_specs=[spec(*w.shape[1:]) for w in weights] + [pl.BlockSpec(memory_space=pl.ANY)] * len(after),
        out_specs=[spec(*o[1:]) for o in outs] + [pl.BlockSpec((8, 128), lambda t: (0, 0))],
        compiler_params=pltpu.CompilerParams(vmem_limit_bytes=VMEM),
        cost_estimate=pl.CostEstimate(flops=us * 10**9, bytes_accessed=10**6, transcendentals=0),
    )(*weights, *after)


def sort_kernel(a_ref, wu, x_ref, up_ref, down_ref, cot_ref, g_ref, st_ref):
    x = nn(to_parity(0), a_ref[...])
    c = nn(to_parity(1), a_ref[...]).astype(BF)
    xb = x.astype(BF)
    x_ref[...] = xb
    for k in range(4):
        for h in range(2):
            at = (2 * h + k // 2) * 128 + (k % 2) * B
            cot_ref[h * B : h * B + B, k * C1 : (k + 1) * C1] = c[at : at + B]
    g = nn(cot_ref[...], wu[...]).astype(BF)
    g_ref[...] = g
    up_ref[0:384, :] = xb[0:384]
    up_ref[384:448, :] = g[0:B, 0:C1]
    up_ref[448:512, :] = g[0:B, C1:C2]
    down_ref[0:384, :] = xb[128:512]
    down_ref[384:448, :] = g[B : 2 * B, 0:C1]
    down_ref[448:512, :] = g[B : 2 * B, C1:C2]
    st_ref[...] = rows8(jnp.sum(x, axis=0, keepdims=True), jnp.sum(x * x, axis=0, keepdims=True))


def forward_kernel(
    edge, x_ref, xd_ref, xu_ref, st_ref, wf, wd,
    ave_ref, avo_ref, low_ref, cact_ref, depth_ref, cv,
    ve, vo, d,
):
    mean, rstd = norm_of(st_ref)
    in_top = jnp.where(edge[0] == 1, 0.0, 1.0)
    in_bot = jnp.where(edge[1] == 1, 0.0, 1.0)

    def latent(row, par):
        ref, base = (xd_ref, row + 3) if row < 0 else (x_ref, row) if row < 4 else (xu_ref, row - 4)
        return ref[base * 128 + par * B : base * 128 + par * B + B, :].astype(F32)

    for row in range(-3, 7):
        at = slice((row + 3) * B, (row + 4) * B)
        for par in range(2):
            z = (latent(row, par) - mean) * rstd
            act = z * sigmoid(z)
            if row < 0:
                act = act * in_top
            if row > 3:
                act = act * in_bot
            ab = act.astype(BF)
            if par == 0:
                ve[at, C1 : 2 * C1] = ab
                vo[at, 0:C1] = ab
                vo[at, 2 * C1 : 3 * C1] = next_col(act).astype(BF)
            else:
                ve[at, 2 * C1 : 3 * C1] = ab
                vo[at, C1 : 2 * C1] = ab
                ve[at, 0:C1] = prev_col(act).astype(BF)

    ave_ref[...] = ve[2 * B : 8 * B, :]
    avo_ref[...] = vo[2 * B : 8 * B, :]
    for par, v in ((0, ve), (1, vo)):
        acc = nn(v[0:512, :], wf[0]) + nn(v[B : B + 512, :], wf[1]) + nn(v[2 * B : 2 * B + 512, :], wf[2])
        for rr in range(8):
            k = 2 * (rr % 2) + par
            r = latent(rr - 2, par) + acc[rr * B : rr * B + B]
            d[(rr // 2) * B : (rr // 2) * B + B, k * C1 : (k + 1) * C1] = r.astype(BF)
    depth_ref[...] = d[B : 3 * B, :]

    low = nn(d[...], wd[...]).astype(BF)
    low_ref[...] = low[B : 3 * B]
    for h in range(4):
        lf = low[h * B : h * B + B].astype(F32)
        ca = lf * sigmoid(lf)
        if h == 0:
            ca = ca * in_top
        if h == 3:
            ca = ca * in_bot
        s = slice(h * B, h * B + B)
        cv[s, 0:C2] = prev_col(ca).astype(BF)
        cv[s, C2 : 2 * C2] = ca.astype(BF)
        cv[s, 2 * C2 : 3 * C2] = next_col(ca).astype(BF)
    cact_ref[...] = cv[B : 3 * B, C2 : 2 * C2]


def coarse_level_kernel(cv, low_ref, depth_ref, wc, wu, send_ref, coarse_ref, ox):
    acc = low_ref[...].astype(F32)
    for i in range(3):
        acc = acc + nn(cv[i * B : i * B + 128, :], wc[i])
    coarse = acc.astype(BF)
    coarse_ref[...] = coarse
    for k in range(4):
        up = nn(coarse, wu[k])
        for h in range(2):
            at = (2 * h + k // 2) * 128 + (k % 2) * B
            o = depth_ref[h * B : h * B + B, k * C1 : (k + 1) * C1].astype(F32) + up[h * B : h * B + B]
            ox[at : at + B, :] = o.astype(BF)
    send_ref[...] = nn(from_parity(), ox[...]).astype(BF)


def gcoarse_kernel(me, g_ref, hd_ref, hu_ref, cact_ref, wc, m0, m1, m2, m3, back_ref, gv):
    gv[B : 3 * B, C2 : 2 * C2] = g_ref[...]
    for s, ref in ((slice(0, B), hd_ref), (slice(3 * B, 4 * B), hu_ref)):
        gv[s, C2 : C2 + C1] = ref[384:448, :]
        gv[s, C2 + C1 : 2 * C2] = ref[448:512, :]
    for h in range(4):
        s = slice(h * B, h * B + B)
        gf = gv[s, C2 : 2 * C2].astype(F32)
        gv[s, 0:C2] = next_col(gf).astype(BF)
        gv[s, 2 * C2 : 3 * C2] = prev_col(gf).astype(BF)
    q = iota((C2, 160), 1)
    core = jnp.where(q >= 80, 1, 0)
    hi = jnp.where(q - 80 * core >= 40, 1, 0)
    channel = (hi * 8 + core) * 40 + q - 80 * core - 40 * hi
    for n, ref in enumerate((m0, m1, m2, m3)):
        pick = one_hot(iota((C2, 160), 0) == channel + lax.rem(me[3] + n, 4) * 80)
        part = nn(gv[:, C2 : 2 * C2], pick).astype(BF)
        ref[:, 0:C2] = cact_ref[...]
        ref[:, C2 : C2 + 160] = part[0:128]
        ref[:, C2 + 160 : C2 + 320] = part[128:256]
    back = None
    for i in (2, 1, 0):
        t = nn(gv[(2 - i) * B : (2 - i) * B + 128, :], wc[i])
        back = t if back is None else back + t
    back_ref[...] = back


def gresid_kernel(cot_ref, g_ref, back_ref, low_ref, wd, gres_ref, geo_ref, glow_ref, up_ref, down_ref):
    glow = g_ref[...].astype(F32) + back_ref[...] * silu_grad(low_ref[...].astype(F32))
    glow = glow.astype(BF)
    glow_ref[...] = glow
    for k in range(4):
        spread = nn(glow, wd[k])
        par = k % 2
        for h in range(2):
            row = 2 * h + k // 2
            s = slice(row * 128 + par * B, row * 128 + par * B + B)
            c = cot_ref[h * B : h * B + B, k * C1 : (k + 1) * C1].astype(F32)
            grb = (c + spread[h * B : h * B + B]).astype(BF)
            gres_ref[s, :] = grb
            geo_ref[par * 256 + row * B : par * 256 + row * B + B, :] = grb
            if row == 0:
                up_ref[par * B : par * B + B, :] = grb
            if row == 3:
                down_ref[par * B : par * B + B, :] = grb


def gnorm_kernel(x_ref, st_ref, geo, hd_ref, hu_ref, wf, gn_ref, st2_ref, rv):
    for row in range(-1, 5):
        to = slice((row + 1) * B, (row + 2) * B)
        for par in range(2):
            ref, at = (hd_ref, 0) if row < 0 else (hu_ref, 0) if row > 3 else (geo, row * B)
            at += par * (256 if 0 <= row < 4 else B)
            grb = ref[at : at + B, :]
            gr = grb.astype(F32)
            rv[1 + par, to, :] = grb
            if par == 0:
                rv[3, to, :] = next_col(gr).astype(BF)
            else:
                rv[0, to, :] = prev_col(gr).astype(BF)
    mean, rstd = norm_of(st_ref)
    s1 = jnp.zeros((1, C1), F32)
    s2 = jnp.zeros((1, C1), F32)
    for par in range(2):
        acc = None
        for i in range(3):
            for j in range(3):
                t = nt(rv[par + 2 - j, (2 - i) * B : (2 - i) * B + 256, :], wf[3 * i + j])
                acc = t if acc is None else acc + t
        for row in range(4):
            s = slice(row * 128 + par * B, row * 128 + par * B + B)
            z = (x_ref[s, :].astype(F32) - mean) * rstd
            gn = acc[row * B : row * B + B] * silu_grad(z)
            gn_ref[s, :] = gn
            s1 = s1 + jnp.sum(gn, axis=0, keepdims=True)
            s2 = s2 + jnp.sum(gn * z, axis=0, keepdims=True)
    st2_ref[...] = rows8(s1, s2)


def grad_latent_kernel(x_ref, st_ref, gn_ref, gres_ref, st2_ref, send_ref, out_ref, token):
    token[...] = jnp.zeros((8, 128), F32)
    mean, rstd = norm_of(st_ref)
    m = group_sums(st2_ref[...]) / COUNT
    z = (x_ref[...].astype(F32) - mean) * rstd
    g = gres_ref[...].astype(F32) + rstd * (gn_ref[...] - m[0:1] - z * m[1:2])
    g = nn(from_parity(), g.astype(BF)).astype(BF)
    for f in range(16):
        out_ref[f, 0:32, :] = send_ref[32 * f : 32 * f + 32, :]
        out_ref[f, 32:64, :] = g[32 * f : 32 * f + 32]


def places(me, rows):
    q = iota((C2, rows), 0)
    core = jnp.where(q >= C1, 1, 0)
    rest = q - C1 * core
    block = (rest * 1639) >> 16
    return ((block & 1) ^ me[5]) * 8 + (block >> 1) * 2 + core, rest - 40 * block


def turn_grads_kernel(me, geo, cot, glow, gt, ct, lt):
    c = iota((C2, C1), 1)
    block, rest = places(me, C1)
    fine = one_hot((rest < 20) & (c == block * 20 + rest))
    up = one_hot((rest >= 20) & (c == block * 20 + rest - 20))
    gt[...] = nt(fine, geo[...]).astype(BF)
    for k in range(4):
        ct[k] = nt(up, cot[:, k * C1 : (k + 1) * C1]).astype(BF)
    block, rest = places(me, C2)
    lt[...] = nt(one_hot(iota((C2, C2), 1) == block * 40 + rest), glow[...]).astype(BF)


def weight_kernel(me, gt, ct, lt, ave, avo, coarse, depth, keep, send, acc):
    for slot, ref in ((0, keep), (1, send)):
        rows = pl.ds(pl.multiple_of((me[2] ^ slot) * C1, 64), C1)
        for i in range(3):
            s = slice(i * B, i * B + 256)
            both = jnp.concatenate([ave[s, :], avo[s, :]], axis=0)
            acc[:, i * 960 : (i + 1) * 960] = nn(gt[rows, :], both)
        for k in range(4):
            s = slice(k * C2, (k + 1) * C2)
            ref[:, s] = (acc[:, s] + nn(ct[k, rows, :], coarse[...])).astype(BF)
        ref[:, 2560:2880] = acc[:, 2560:2880].astype(BF)
        ref[:, 2880:2944] = jnp.zeros((C1, 64), BF)
        ref[:, 2944:4224] = nn(lt[rows, :], depth[...]).astype(BF)


def coarse_kernel(me, m0, m1, m2, m3, keep, send, a, res):
    eye = one_hot(iota((160, 160), 0) == iota((160, 160), 1))
    lane = iota((160, 256), 1) & 63
    for s, ref in enumerate((m0, m1, m2, m3)):
        f = nt(eye, jnp.concatenate([ref[:, C2 : C2 + 160], ref[:, C2 + 160 : C2 + 320]], axis=0))
        taps = (
            jnp.where(lane == 63, 0.0, pltpu.roll(f, 255, 1)),
            f,
            jnp.where(lane == 0, 0.0, pltpu.roll(f, 1, 1)),
        )
        at = slice(s * 128, s * 128 + 128)
        for j, v in enumerate(taps):
            mid = pltpu.roll(v, 192, 1)
            a[j * 160 : j * 160 + 160, at] = v[:, 128:256].astype(BF)
            a[(3 + j) * 160 : (3 + j) * 160 + 160, at] = mid[:, 0:128].astype(BF)
            a[(6 + j) * 160 : (6 + j) * 160 + 160, at] = v[:, 0:128].astype(BF)
    act = jnp.concatenate([m0[:, 0:C2], m1[:, 0:C2], m2[:, 0:C2], m3[:, 0:C2]], axis=0)
    res[...] = nn(a[...], act)
    for slot, ref in ((0, keep), (1, send)):
        for t in range(9):
            for e in range(2):
                at = t * 160 + (me[2] ^ slot) * 80 + (me[5] ^ e) * 40
                v = res[pl.ds(pl.multiple_of(at, 8), 40), :].astype(BF)
                for i in range(8):
                    to = lax.rem(i // 2 + 4 - me[0], 4) * 4 + ((i % 2) ^ me[1]) * 2 + e
                    ref[to, :, t * 80 : t * 80 + 80] = v[:, i * 80 : i * 80 + 80]


def pack_kernel(me, a_ref, o0, o1, o2, o3, acc, low, high, out):
    acc[...] = (a_ref[0].astype(F32) + a_ref[1].astype(F32)) + (a_ref[2].astype(F32) + a_ref[3].astype(F32))
    low[...] = jnp.zeros(low.shape, F32)
    high[...] = jnp.zeros(high.shape, F32)
    row = iota((80, 384), 0)
    first = jnp.where(row >= 40, row - 40, row) < 20
    for i in range(8):
        for t in range(9):
            low[:, t * 40 : t * 40 + 40] = acc[:, t * C1 + i * 40 : t * C1 + i * 40 + 40]
        for k in range(4):
            high[:, k * 80 : k * 80 + 80] = acc[:, k * C2 + i * 80 : k * C2 + i * 80 + 80]
        to = lax.rem(i // 2 + 4 - me[0], 4) * 2 + ((i % 2) ^ me[1])
        out[to, :, 0:384] = jnp.where(first, low[:, 0:384], high[:, 0:384]).astype(BF)
        for k in range(4):
            at = 2944 + k * C1 + i * 40
            high[:, 384 + k * 40 : 424 + k * 40] = acc[:, at : at + 40]
        out[to, :, 384:640] = high[:, 384:640].astype(BF)
    for n, ref in enumerate((o0, o1, o2, o3)):
        ref[...] = out[2 * n : 2 * n + 2]


def join_kernel(a, b, c, d, coarse, *outs):
    for n, ref in enumerate(outs):
        s = slice(n % 2 * 40, n % 2 * 40 + 40)
        total = a[n // 2, s, :].astype(F32) + b[n // 2, s, :].astype(F32)
        total = total + c[n // 2, s, :].astype(F32) + d[n // 2, s, :].astype(F32)
        ref[:, 0:C2] = total.astype(BF)
        ref[:, C2:] = coarse[n]


def finish_kernel(scale, a_ref, b_ref, c_ref, d_ref, fine_ref, down_ref, coarse_ref, up_ref, u):
    total = a_ref[...].astype(F32) + b_ref[...].astype(F32)
    total = (total + c_ref[...].astype(F32) + d_ref[...].astype(F32)) * scale
    for t in range(9):
        fine_ref[t] = total[0:20, t * 40 : t * 40 + 40]
    u[...] = jnp.zeros(u.shape, F32)
    for k in range(4):
        up_ref[:, k, :] = total[20:40, k * 80 : k * 80 + 80]
        u[0:40, 0:40] = total[:, 384 + k * 40 : 424 + k * 40]
        down_ref[k] = jnp.transpose(u[...])[0:40, 0:40]
    for t in range(9):
        coarse_ref[t] = total[:, C2 + t * 80 : C2 + t * 80 + 80]


def pair_kernel(mine, got, *outs):
    for n, ref in enumerate(outs):
        s = slice(4 * n, 4 * n + 4)
        ref[...] = (mine[s].astype(F32) + got[s].astype(F32)).astype(BF)


def slab_kernel(mine, got, st, out_ref, st_ref):
    st_ref[...] = st[...]
    for n in range(8):
        out_ref[n] = (mine[n].astype(F32) + got[n].astype(F32)).astype(BF)


def add(*terms):
    total = terms[0].astype(F32)
    for t in terms[1:]:
        total = total + t.astype(F32)
    return total.astype(BF)


def other_core(v):
    return lax.ppermute(v, "wa", [(w, w ^ 1) for w in range(16)])


def ring_x(v, step):
    return lax.ppermute(v, "ha", [(h, ((h // 2 + step) % 4) * 2 + h % 2) for h in range(8)])


def other_y(v):
    return lax.ppermute(v, "ha", [(h, h ^ 1) for h in range(8)])


def ring_z(v, step):
    return lax.ppermute(
        v, "wa", [(w, (w // 8) * 8 + ((w // 2 + step) % 4) * 2 + w % 2) for w in range(16)]
    )


def other_y_hi(v):
    return lax.ppermute(v, "wa", [(w, w ^ 8) for w in range(16)])


def to_next(v):
    return lax.ppermute(v, "ha", [(h, h + 1) for h in range(7)])


def to_prev(v):
    return lax.ppermute(v, "ha", [(h + 1, h) for h in range(7)])


def swap_wa(v):
    return lax.all_to_all(v, "wa", 0, 0, tiled=True)


def other_both(v):
    pairs = [(h * 16 + w, (h ^ 1) * 16 + (w ^ 8)) for h in range(8) for w in range(16)]
    return lax.ppermute(v, ("ha", "wa"), pairs)


def swap_z(v):
    groups = [[hi * 8 + z * 2 + core for z in range(4)] for hi in range(2) for core in range(2)]
    return lax.all_to_all(v, "wa", 0, 0, axis_index_groups=groups, tiled=True)


def shards(latent, cotangent, w_fine, w_down, w_coarse, w_up):
    ha, wa = (lax.axis_index("ha"), lax.axis_index("wa"))
    edge = jnp.stack([ha == 0, ha == 7]).astype(jnp.int32)
    me = jnp.stack([ha // 2, ha % 2, wa % 2, (wa // 2) % 4, wa, wa // 8]).astype(jnp.int32)
    frames, rows, cols, _ = latent.shape
    scale = float(frames * 32 * 128) ** (-0.5)
    up_t = jnp.swapaxes(w_up, 1, 2)

    lat = latent.reshape(16, 32, C1)
    both = swap_wa(jnp.concatenate([lat, cotangent.reshape(16, 32, C1)], axis=1))
    wct, token = turned([w_coarse], 9)
    x, up, down, cotk, g, st = call(
        sort_kernel,
        [
            sds((512, C1)),
            sds((512, C1)),
            sds((512, C1)),
            sds((128, 4 * C1)),
            sds((128, C2)),
            sds((8, C1), F32),
        ],
        2,
        us=4,
        after=(token,),
    )(both.reshape(1024, C1), up_t.reshape(4 * C1, C2))
    st_y = st + other_y(st)
    st = st_y + ring_x(st_y, 1) + ring_x(st_y, 2) + ring_x(st_y, 3)
    hd, hu = (to_next(down), to_prev(up))

    wdt, wun, _ = turned([w_down, up_t], 4, after=(st_y,))
    ave, avo, low, cact, depth, cv = call(
        forward_kernel,
        [
            sds((384, 3 * C1)),
            sds((384, 3 * C1)),
            sds((128, C2)),
            sds((128, C2)),
            sds((128, 4 * C1)),
            sds((256, 3 * C2)),
        ],
        6,
        [pltpu.VMEM((640, 3 * C1), BF), pltpu.VMEM((640, 3 * C1), BF), pltpu.VMEM((256, 4 * C1), BF)],
        smem=1,
        us=7,
    )(edge, x, hd, hu, st, w_fine.reshape(3, 3 * C1, C1), w_down.reshape(4 * C1, C2))
    send, coarse = call(
        coarse_level_kernel,
        [sds((512, C1)), sds((128, C2))],
        5,
        [pltpu.VMEM((512, C1), BF)],
        us=3,
    )(cv, low, depth, w_coarse.reshape(3, 3 * C2, C2), wun)

    m0, m1, m2, m3, back = call(
        gcoarse_kernel,
        [sds((128, 960))] * 4 + [sds((128, C2), F32)],
        5,
        [pltpu.VMEM((256, 3 * C2), BF)],
        smem=1,
        us=6,
    )(me, g, hd, hu, cact, wct.reshape(3, 3 * C2, C2))
    m1, m2, m3 = (ring_z(v, n + 1) for n, v in enumerate((m1, m2, m3)))

    gres, geo, glow, up, down = call(
        gresid_kernel,
        [sds((512, C1)), sds((512, C1)), sds((128, C2)), sds((128, C1)), sds((128, C1))],
        5,
        us=3,
    )(cotk, g, back, low, wdt)
    ed, eu = (to_next(down), to_prev(up))

    gt, ct, lt = call(
        turn_grads_kernel,
        [sds((C2, 512)), sds((4, C2, 128)), sds((C2, 128))],
        3,
        smem=1,
        us=3,
        after=(m1[:8, :128] + m2[:8, :128] + m3[:8, :128],),
    )(me, geo, cotk, glow)
    kw, sw = call(
        weight_kernel,
        [sds((C1, 4224))] * 2,
        7,
        [pltpu.VMEM((C1, 2880), F32)],
        smem=1,
        us=7,
        after=(ed, eu),
    )(me, gt, ct, lt, ave, avo, coarse, depth)
    got_w = other_core(sw)
    gn, st2 = call(
        gnorm_kernel,
        [sds((512, C1), F32), sds((8, C1), F32)],
        6,
        [pltpu.VMEM((4, 384, C1), BF)],
        us=6,
        after=(sw,),
    )(x, st, geo, ed, eu, w_fine)
    pair_w, st2 = call(slab_kernel, [sds((8, 40, 4224)), sds((8, C1), F32)], 3, us=4)(
        kw.reshape(8, 40, 4224), got_w.reshape(8, 40, 4224), st2
    )
    sums_w = swap_z(pair_w.reshape(4, 80, 4224))
    st2_y = st2 + other_y(st2)
    st2 = st2_y + ring_x(st2_y, 1) + ring_x(st2_y, 2) + ring_x(st2_y, 3)
    kc, sc = call(
        coarse_kernel,
        [sds((16, 40, 720))] * 2,
        4,
        [pltpu.VMEM((1440, 512), BF), pltpu.VMEM((1440, C2), F32)],
        smem=1,
        us=1,
        after=(st2_y,),
    )(me, m0, m1, m2, m3)
    got_c = other_core(sc)

    pair_c = call(pair_kernel, [sds((4, 40, 720))] * 4, 2, us=1, after=(st2_y,))(kc, got_c)
    coarse_x = add(pair_c[0], *[ring_x(pair_c[n], n) for n in range(1, 4)])

    gsend, token = call(grad_latent_kernel, [sds((16, 64, C1)), sds((8, 128), F32)], 6, us=1, after=(coarse_x[0, :8, :128],))(
        x, st, gn, gres, st2, send
    )
    home = swap_wa(gsend)
    output = home[:, :32].reshape(frames, rows, cols, C1)
    grad_latent = home[:, 32:].reshape(frames, rows, cols, C1)

    packed = call(
        pack_kernel,
        [sds((2, 80, C2))] * 4,
        1,
        [
            pltpu.VMEM((80, 4224), F32),
            pltpu.VMEM((80, C2), F32),
            pltpu.VMEM((80, C2), F32),
            pltpu.VMEM((8, 80, C2), BF),
        ],
        smem=1,
        us=0,
        after=(coarse_x, token),
    )(me, sums_w)
    joined = call(join_kernel, [sds((40, 1360))] * 4, 5, us=0, after=(home[0, :8, :128],))(
        packed[0], *[ring_x(packed[n], n) for n in range(1, 4)], coarse_x
    )
    fine, down, coarse_w, up = call(
        functools.partial(finish_kernel, scale),
        [sds((9, 20, 40), F32), sds((4, 40, 40), F32), sds((9, 40, 80), F32), sds((20, 4, 80), F32)],
        4,
        [pltpu.VMEM((128, 128), F32)],
    )(joined[0], other_y(joined[2]), other_y_hi(joined[1]), other_both(joined[3]))
    fine, coarse_w = (jnp.swapaxes(v, 1, 2) for v in (fine, coarse_w))
    return output, grad_latent, fine, down, coarse_w, jnp.transpose(up, (1, 2, 0))


def solution(mesh):
    big, small = (P(None, "ha", "wa", None), P(None, "ha", "wa"))
    return jax.shard_map(
        shards,
        mesh=mesh,
        in_specs=(big, big, P(), P(), P(), P()),
        out_specs=(big, big, small, small, small, small),
        check_vma=False,
    )
```

```python
import functools

import jax
import jax.numpy as jnp
from jax import lax
from jax.experimental import pallas as pl
from jax.experimental.pallas import tpu as pltpu
from jax.sharding import PartitionSpec as P


BF = jnp.bfloat16
F32 = jnp.float32
EPS = 1e-05
C1, C2 = 320, 640
B = 64
COUNT = 32.0 * 128.0 * 10.0
VMEM = 16 * 1024 * 1024


def nn(a, b):
    return lax.dot_general(a, b, (((1,), (0,)), ((), ())), preferred_element_type=F32)


def nt(a, b):
    return lax.dot_general(a, b, (((1,), (1,)), ((), ())), preferred_element_type=F32)


def tn(a, b):
    return lax.dot_general(a, b, (((0,), (0,)), ((), ())), preferred_element_type=F32)


def iota(shape, dim):
    return lax.broadcasted_iota(jnp.int32, shape, dim)


def one_hot(cond):
    return jnp.where(cond, 1.0, 0.0).astype(BF)


def arrival_of(q):
    row, par, col = (q >> 7, (q >> 6) & 1, q & 63)
    return ((col >> 2) << 5) + (row << 3) + ((col & 3) << 1) + par


def to_parity(which):
    q, a = (iota((512, 1024), 0), iota((512, 1024), 1))
    return one_hot((arrival_of(q) == ((a >> 6) << 5) + (a & 31)) & (((a >> 5) & 1) == which))


def from_parity():
    return one_hot(arrival_of(iota((512, 512), 1)) == iota((512, 512), 0))


def prev_col(v):
    return jnp.where(iota(v.shape, 0) == 0, 0.0, pltpu.roll(v, 1, 0))


def next_col(v):
    return jnp.where(iota(v.shape, 0) == B - 1, 0.0, pltpu.roll(v, B - 1, 0))


def group_sums(sums):
    same = ((iota((C1, C1), 0) * 6554) >> 16) == ((iota((C1, C1), 1) * 6554) >> 16)
    return lax.dot_general(
        sums,
        jnp.where(same, 1.0, 0.0).astype(F32),
        (((1,), (0,)), ((), ())),
        precision=lax.Precision.HIGHEST,
        preferred_element_type=F32,
    )


def group_sums(sums):
    same = ((iota((C1, C1), 0) * 6554) >> 16) == ((iota((C1, C1), 1) * 6554) >> 16)
    return lax.dot_general(
        sums,
        jnp.where(same, 1.0, 0.0).astype(F32),
        (((1,), (0,)), ((), ())),
        precision=lax.Precision.HIGHEST,
        preferred_element_type=F32,
    )


def norm_of(st_ref):
    totals = group_sums(st_ref[...]) / COUNT
    mean = totals[0:1]
    return mean, lax.rsqrt(totals[1:2] - mean * mean + EPS)


def sigmoid(v):
    return 1.0 / (1.0 + jnp.exp(-v))


def silu_grad(v):
    s = sigmoid(v)
    return s * (1.0 + v * (1.0 - s))


def rows8(a, b):
    return jnp.concatenate([a, b, jnp.zeros((6, a.shape[1]), F32)], axis=0)


def call(kernel, outs, n_in, scratch=(), smem=0, us=2, after=(), vmem=VMEM):
    first = smem + n_in

    def body(*refs):
        kernel(*refs[:first], *refs[first + len(after) :])

    f = pl.pallas_call(
        body,
        out_shape=outs,
        in_specs=[pl.BlockSpec(memory_space=pltpu.SMEM)] * smem
        + [pl.BlockSpec(memory_space=pltpu.VMEM)] * n_in
        + [pl.BlockSpec(memory_space=pl.ANY)] * len(after),
        out_specs=jax.tree.map(lambda _: pl.BlockSpec(memory_space=pltpu.VMEM), outs),
        scratch_shapes=list(scratch),
        compiler_params=pltpu.CompilerParams(vmem_limit_bytes=vmem),
        cost_estimate=pl.CostEstimate(flops=us * 10**9, bytes_accessed=10**6, transcendentals=0),
    )
    return lambda *args: f(*args, *after)


def sds(shape, dtype=BF):
    return jax.ShapeDtypeStruct(shape, dtype)


def turn_kernel(count, *refs):
    for src, dst in zip(refs[:count], refs[-count - 1 : -1]):
        dst[0] = jnp.transpose(src[0])
    refs[-1][...] = jnp.zeros((8, 128), F32)


def turned(weights, us, after=()):
    def spec(rows, cols):
        return pl.BlockSpec((1, rows, cols), lambda t: (t, 0, 0))

    outs = [(w.shape[0], w.shape[2], w.shape[1]) for w in weights]
    return pl.pallas_call(
        functools.partial(turn_kernel, len(weights)),
        grid=(weights[0].shape[0],),
        out_shape=[sds(o) for o in outs] + [sds((8, 128), F32)],
        in_specs=[spec(*w.shape[1:]) for w in weights] + [pl.BlockSpec(memory_space=pl.ANY)] * len(after),
        out_specs=[spec(*o[1:]) for o in outs] + [pl.BlockSpec((8, 128), lambda t: (0, 0))],
        compiler_params=pltpu.CompilerParams(vmem_limit_bytes=VMEM),
        cost_estimate=pl.CostEstimate(flops=us * 10**9, bytes_accessed=10**6, transcendentals=0),
    )(*weights, *after)


def sort_kernel(a_ref, wu, x_ref, up_ref, down_ref, cot_ref, g_ref, st_ref):
    x = nn(to_parity(0), a_ref[...])
    c = nn(to_parity(1), a_ref[...]).astype(BF)
    xb = x.astype(BF)
    x_ref[...] = xb
    for k in range(4):
        for h in range(2):
            at = (2 * h + k // 2) * 128 + (k % 2) * B
            cot_ref[h * B : h * B + B, k * C1 : (k + 1) * C1] = c[at : at + B]
    g = nn(cot_ref[...], wu[...]).astype(BF)
    g_ref[...] = g
    up_ref[0:384, :] = xb[0:384]
    up_ref[384:448, :] = g[0:B, 0:C1]
    up_ref[448:512, :] = g[0:B, C1:C2]
    down_ref[0:384, :] = xb[128:512]
    down_ref[384:448, :] = g[B : 2 * B, 0:C1]
    down_ref[448:512, :] = g[B : 2 * B, C1:C2]
    st_ref[...] = rows8(jnp.sum(x, axis=0, keepdims=True), jnp.sum(x * x, axis=0, keepdims=True))


def forward_kernel(
    edge, x_ref, xd_ref, xu_ref, st_ref, wf, wd,
    ave_ref, avo_ref, low_ref, cact_ref, depth_ref, cv,
    ve, vo, d,
):
    mean, rstd = norm_of(st_ref)
    in_top = jnp.where(edge[0] == 1, 0.0, 1.0)
    in_bot = jnp.where(edge[1] == 1, 0.0, 1.0)

    def latent(row, par):
        ref, base = (xd_ref, row + 3) if row < 0 else (x_ref, row) if row < 4 else (xu_ref, row - 4)
        return ref[base * 128 + par * B : base * 128 + par * B + B, :].astype(F32)

    for row in range(-3, 7):
        at = slice((row + 3) * B, (row + 4) * B)
        for par in range(2):
            z = (latent(row, par) - mean) * rstd
            act = z * sigmoid(z)
            if row < 0:
                act = act * in_top
            if row > 3:
                act = act * in_bot
            ab = act.astype(BF)
            if par == 0:
                ve[at, C1 : 2 * C1] = ab
                vo[at, 0:C1] = ab
                vo[at, 2 * C1 : 3 * C1] = next_col(act).astype(BF)
            else:
                ve[at, 2 * C1 : 3 * C1] = ab
                vo[at, C1 : 2 * C1] = ab
                ve[at, 0:C1] = prev_col(act).astype(BF)

    ave_ref[...] = ve[2 * B : 8 * B, :]
    avo_ref[...] = vo[2 * B : 8 * B, :]
    for par, v in ((0, ve), (1, vo)):
        acc = nn(v[0:512, :], wf[0]) + nn(v[B : B + 512, :], wf[1]) + nn(v[2 * B : 2 * B + 512, :], wf[2])
        for rr in range(8):
            k = 2 * (rr % 2) + par
            r = latent(rr - 2, par) + acc[rr * B : rr * B + B]
            d[(rr // 2) * B : (rr // 2) * B + B, k * C1 : (k + 1) * C1] = r.astype(BF)
    depth_ref[...] = d[B : 3 * B, :]

    low = nn(d[...], wd[...]).astype(BF)
    low_ref[...] = low[B : 3 * B]
    for h in range(4):
        lf = low[h * B : h * B + B].astype(F32)
        ca = lf * sigmoid(lf)
        if h == 0:
            ca = ca * in_top
        if h == 3:
            ca = ca * in_bot
        s = slice(h * B, h * B + B)
        cv[s, 0:C2] = prev_col(ca).astype(BF)
        cv[s, C2 : 2 * C2] = ca.astype(BF)
        cv[s, 2 * C2 : 3 * C2] = next_col(ca).astype(BF)
    cact_ref[...] = cv[B : 3 * B, C2 : 2 * C2]


def coarse_level_kernel(cv, low_ref, depth_ref, wc, wu, send_ref, coarse_ref, ox):
    acc = low_ref[...].astype(F32)
    for i in range(3):
        acc = acc + nn(cv[i * B : i * B + 128, :], wc[i])
    coarse = acc.astype(BF)
    coarse_ref[...] = coarse
    for k in range(4):
        up = nn(coarse, wu[k])
        for h in range(2):
            at = (2 * h + k // 2) * 128 + (k % 2) * B
            o = depth_ref[h * B : h * B + B, k * C1 : (k + 1) * C1].astype(F32) + up[h * B : h * B + B]
            ox[at : at + B, :] = o.astype(BF)
    send_ref[...] = nn(from_parity(), ox[...]).astype(BF)


def gcoarse_kernel(me, g_ref, hd_ref, hu_ref, cact_ref, wc, m0, m1, m2, m3, back_ref, gv):
    gv[B : 3 * B, C2 : 2 * C2] = g_ref[...]
    for s, ref in ((slice(0, B), hd_ref), (slice(3 * B, 4 * B), hu_ref)):
        gv[s, C2 : C2 + C1] = ref[384:448, :]
        gv[s, C2 + C1 : 2 * C2] = ref[448:512, :]
    for h in range(4):
        s = slice(h * B, h * B + B)
        gf = gv[s, C2 : 2 * C2].astype(F32)
        gv[s, 0:C2] = next_col(gf).astype(BF)
        gv[s, 2 * C2 : 3 * C2] = prev_col(gf).astype(BF)
    q = iota((C2, 160), 1)
    core = jnp.where(q >= 80, 1, 0)
    hi = jnp.where(q - 80 * core >= 40, 1, 0)
    channel = (hi * 8 + core) * 40 + q - 80 * core - 40 * hi
    for n, ref in enumerate((m0, m1, m2, m3)):
        pick = one_hot(iota((C2, 160), 0) == channel + lax.rem(me[3] + n, 4) * 80)
        part = nn(gv[:, C2 : 2 * C2], pick).astype(BF)
        ref[:, 0:C2] = cact_ref[...]
        ref[:, C2 : C2 + 160] = part[0:128]
        ref[:, C2 + 160 : C2 + 320] = part[128:256]
    back = None
    for i in (2, 1, 0):
        t = nn(gv[(2 - i) * B : (2 - i) * B + 128, :], wc[i])
        back = t if back is None else back + t
    back_ref[...] = back


def gresid_kernel(cot_ref, g_ref, back_ref, low_ref, wd, gres_ref, geo_ref, glow_ref, up_ref, down_ref):
    glow = g_ref[...].astype(F32) + back_ref[...] * silu_grad(low_ref[...].astype(F32))
    glow = glow.astype(BF)
    glow_ref[...] = glow
    for k in range(4):
        spread = nn(glow, wd[k])
        par = k % 2
        for h in range(2):
            row = 2 * h + k // 2
            s = slice(row * 128 + par * B, row * 128 + par * B + B)
            c = cot_ref[h * B : h * B + B, k * C1 : (k + 1) * C1].astype(F32)
            grb = (c + spread[h * B : h * B + B]).astype(BF)
            gres_ref[s, :] = grb
            geo_ref[par * 256 + row * B : par * 256 + row * B + B, :] = grb
            if row == 0:
                up_ref[par * B : par * B + B, :] = grb
            if row == 3:
                down_ref[par * B : par * B + B, :] = grb


def gnorm_kernel(x_ref, st_ref, geo, hd_ref, hu_ref, wf, gn_ref, st2_ref, rv):
    for row in range(-1, 5):
        to = slice((row + 1) * B, (row + 2) * B)
        for par in range(2):
            ref, at = (hd_ref, 0) if row < 0 else (hu_ref, 0) if row > 3 else (geo, row * B)
            at += par * (256 if 0 <= row < 4 else B)
            grb = ref[at : at + B, :]
            gr = grb.astype(F32)
            rv[1 + par, to, :] = grb
            if par == 0:
                rv[3, to, :] = next_col(gr).astype(BF)
            else:
                rv[0, to, :] = prev_col(gr).astype(BF)
    mean, rstd = norm_of(st_ref)
    s1 = jnp.zeros((1, C1), F32)
    s2 = jnp.zeros((1, C1), F32)
    for par in range(2):
        acc = None
        for i in range(3):
            for j in range(3):
                t = nt(rv[par + 2 - j, (2 - i) * B : (2 - i) * B + 256, :], wf[3 * i + j])
                acc = t if acc is None else acc + t
        for row in range(4):
            s = slice(row * 128 + par * B, row * 128 + par * B + B)
            z = (x_ref[s, :].astype(F32) - mean) * rstd
            gn = acc[row * B : row * B + B] * silu_grad(z)
            gn_ref[s, :] = gn
            s1 = s1 + jnp.sum(gn, axis=0, keepdims=True)
            s2 = s2 + jnp.sum(gn * z, axis=0, keepdims=True)
    st2_ref[...] = rows8(s1, s2)


def grad_latent_kernel(x_ref, st_ref, gn_ref, gres_ref, st2_ref, send_ref, out_ref, token):
    token[...] = jnp.zeros((8, 128), F32)
    mean, rstd = norm_of(st_ref)
    m = group_sums(st2_ref[...]) / COUNT
    z = (x_ref[...].astype(F32) - mean) * rstd
    g = gres_ref[...].astype(F32) + rstd * (gn_ref[...] - m[0:1] - z * m[1:2])
    g = nn(from_parity(), g.astype(BF)).astype(BF)
    for f in range(16):
        out_ref[f, 0:32, :] = send_ref[32 * f : 32 * f + 32, :]
        out_ref[f, 32:64, :] = g[32 * f : 32 * f + 32]


def places(me, rows):
    q = iota((C2, rows), 0)
    core = jnp.where(q >= C1, 1, 0)
    rest = q - C1 * core
    block = (rest * 1639) >> 16
    return ((block & 1) ^ me[5]) * 8 + (block >> 1) * 2 + core, rest - 40 * block


def turn_grads_kernel(me, geo, cot, glow, gt, ct, lt):
    c = iota((C2, C1), 1)
    block, rest = places(me, C1)
    fine = one_hot((rest < 20) & (c == block * 20 + rest))
    up = one_hot((rest >= 20) & (c == block * 20 + rest - 20))
    gt[...] = nt(fine, geo[...]).astype(BF)
    for k in range(4):
        ct[k] = nt(up, cot[:, k * C1 : (k + 1) * C1]).astype(BF)
    block, rest = places(me, C2)
    lt[...] = nt(one_hot(iota((C2, C2), 1) == block * 40 + rest), glow[...]).astype(BF)


def weight_kernel(me, gt, ct, lt, ave, avo, coarse, depth, keep, send, acc):
    for slot, ref in ((0, keep), (1, send)):
        rows = pl.ds(pl.multiple_of((me[2] ^ slot) * C1, 64), C1)
        for i in range(3):
            s = slice(i * B, i * B + 256)
            both = jnp.concatenate([ave[s, :], avo[s, :]], axis=0)
            acc[:, i * 960 : (i + 1) * 960] = nn(gt[rows, :], both)
        for k in range(4):
            s = slice(k * C2, (k + 1) * C2)
            ref[:, s] = (acc[:, s] + nn(ct[k, rows, :], coarse[...])).astype(BF)
        ref[:, 2560:2880] = acc[:, 2560:2880].astype(BF)
        ref[:, 2880:2944] = jnp.zeros((C1, 64), BF)
        ref[:, 2944:4224] = nn(lt[rows, :], depth[...]).astype(BF)


def coarse_kernel(me, m0, m1, m2, m3, keep, send, a, res):
    eye = one_hot(iota((160, 160), 0) == iota((160, 160), 1))
    lane = iota((160, 256), 1) & 63
    for s, ref in enumerate((m0, m1, m2, m3)):
        f = nt(eye, jnp.concatenate([ref[:, C2 : C2 + 160], ref[:, C2 + 160 : C2 + 320]], axis=0))
        taps = (
            jnp.where(lane == 63, 0.0, pltpu.roll(f, 255, 1)),
            f,
            jnp.where(lane == 0, 0.0, pltpu.roll(f, 1, 1)),
        )
        at = slice(s * 128, s * 128 + 128)
        for j, v in enumerate(taps):
            mid = pltpu.roll(v, 192, 1)
            a[j * 160 : j * 160 + 160, at] = v[:, 128:256].astype(BF)
            a[(3 + j) * 160 : (3 + j) * 160 + 160, at] = mid[:, 0:128].astype(BF)
            a[(6 + j) * 160 : (6 + j) * 160 + 160, at] = v[:, 0:128].astype(BF)
    act = jnp.concatenate([m0[:, 0:C2], m1[:, 0:C2], m2[:, 0:C2], m3[:, 0:C2]], axis=0)
    res[...] = nn(a[...], act)
    for slot, ref in ((0, keep), (1, send)):
        for t in range(9):
            for e in range(2):
                at = t * 160 + (me[2] ^ slot) * 80 + (me[5] ^ e) * 40
                v = res[pl.ds(pl.multiple_of(at, 8), 40), :].astype(BF)
                for i in range(8):
                    to = lax.rem(i // 2 + 4 - me[0], 4) * 4 + ((i % 2) ^ me[1]) * 2 + e
                    ref[to, :, t * 80 : t * 80 + 80] = v[:, i * 80 : i * 80 + 80]


def pack_kernel(me, a_ref, o0, o1, o2, o3, acc, low, high, out):
    acc[...] = (a_ref[0].astype(F32) + a_ref[1].astype(F32)) + (a_ref[2].astype(F32) + a_ref[3].astype(F32))
    low[...] = jnp.zeros(low.shape, F32)
    high[...] = jnp.zeros(high.shape, F32)
    row = iota((80, 384), 0)
    first = jnp.where(row >= 40, row - 40, row) < 20
    for i in range(8):
        for t in range(9):
            low[:, t * 40 : t * 40 + 40] = acc[:, t * C1 + i * 40 : t * C1 + i * 40 + 40]
        for k in range(4):
            high[:, k * 80 : k * 80 + 80] = acc[:, k * C2 + i * 80 : k * C2 + i * 80 + 80]
        to = lax.rem(i // 2 + 4 - me[0], 4) * 2 + ((i % 2) ^ me[1])
        out[to, :, 0:384] = jnp.where(first, low[:, 0:384], high[:, 0:384]).astype(BF)
        for k in range(4):
            at = 2944 + k * C1 + i * 40
            high[:, 384 + k * 40 : 424 + k * 40] = acc[:, at : at + 40]
        out[to, :, 384:640] = high[:, 384:640].astype(BF)
    for n, ref in enumerate((o0, o1, o2, o3)):
        ref[...] = out[2 * n : 2 * n + 2]


def join_kernel(a, b, c, d, coarse, *outs):
    for n, ref in enumerate(outs):
        s = slice(n % 2 * 40, n % 2 * 40 + 40)
        total = a[n // 2, s, :].astype(F32) + b[n // 2, s, :].astype(F32)
        total = total + c[n // 2, s, :].astype(F32) + d[n // 2, s, :].astype(F32)
        ref[:, 0:C2] = total.astype(BF)
        ref[:, C2:] = coarse[n]


def finish_kernel(scale, a_ref, b_ref, c_ref, d_ref, fine_ref, down_ref, coarse_ref, up_ref, u):
    total = a_ref[...].astype(F32) + b_ref[...].astype(F32)
    total = (total + c_ref[...].astype(F32) + d_ref[...].astype(F32)) * scale
    for t in range(9):
        fine_ref[t] = total[0:20, t * 40 : t * 40 + 40]
    u[...] = jnp.zeros(u.shape, F32)
    for k in range(4):
        up_ref[:, k, :] = total[20:40, k * 80 : k * 80 + 80]
        u[0:40, 0:40] = total[:, 384 + k * 40 : 424 + k * 40]
        down_ref[k] = jnp.transpose(u[...])[0:40, 0:40]
    for t in range(9):
        coarse_ref[t] = total[:, C2 + t * 80 : C2 + t * 80 + 80]


def pair_kernel(mine, got, *outs):
    for n, ref in enumerate(outs):
        s = slice(4 * n, 4 * n + 4)
        ref[...] = (mine[s].astype(F32) + got[s].astype(F32)).astype(BF)


def slab_kernel(mine, got, st, out_ref, st_ref):
    st_ref[...] = st[...]
    for n in range(8):
        out_ref[n] = (mine[n].astype(F32) + got[n].astype(F32)).astype(BF)


def add(*terms):
    total = terms[0].astype(F32)
    for t in terms[1:]:
        total = total + t.astype(F32)
    return total.astype(BF)


def other_core(v):
    return lax.ppermute(v, "wa", [(w, w ^ 1) for w in range(16)])


def ring_x(v, step):
    return lax.ppermute(v, "ha", [(h, ((h // 2 + step) % 4) * 2 + h % 2) for h in range(8)])


def other_y(v):
    return lax.ppermute(v, "ha", [(h, h ^ 1) for h in range(8)])


def ring_z(v, step):
    return lax.ppermute(
        v, "wa", [(w, (w // 8) * 8 + ((w // 2 + step) % 4) * 2 + w % 2) for w in range(16)]
    )


def other_y_hi(v):
    return lax.ppermute(v, "wa", [(w, w ^ 8) for w in range(16)])


def to_next(v):
    return lax.ppermute(v, "ha", [(h, h + 1) for h in range(7)])


def to_prev(v):
    return lax.ppermute(v, "ha", [(h + 1, h) for h in range(7)])


def swap_wa(v):
    return lax.all_to_all(v, "wa", 0, 0, tiled=True)


def other_both(v):
    pairs = [(h * 16 + w, (h ^ 1) * 16 + (w ^ 8)) for h in range(8) for w in range(16)]
    return lax.ppermute(v, ("ha", "wa"), pairs)


def swap_z(v):
    groups = [[hi * 8 + z * 2 + core for z in range(4)] for hi in range(2) for core in range(2)]
    return lax.all_to_all(v, "wa", 0, 0, axis_index_groups=groups, tiled=True)


def shards(latent, cotangent, w_fine, w_down, w_coarse, w_up):
    ha, wa = (lax.axis_index("ha"), lax.axis_index("wa"))
    edge = jnp.stack([ha == 0, ha == 7]).astype(jnp.int32)
    me = jnp.stack([ha // 2, ha % 2, wa % 2, (wa // 2) % 4, wa, wa // 8]).astype(jnp.int32)
    frames, rows, cols, _ = latent.shape
    scale = float(frames * 32 * 128) ** (-0.5)
    up_t = jnp.swapaxes(w_up, 1, 2)

    lat = latent.reshape(16, 32, C1)
    both = swap_wa(jnp.concatenate([lat, cotangent.reshape(16, 32, C1)], axis=1))
    wct, token = turned([w_coarse], 9)
    x, up, down, cotk, g, st = call(
        sort_kernel,
        [
            sds((512, C1)),
            sds((512, C1)),
            sds((512, C1)),
            sds((128, 4 * C1)),
            sds((128, C2)),
            sds((8, C1), F32),
        ],
        2,
        us=4,
        after=(token,),
    )(both.reshape(1024, C1), up_t.reshape(4 * C1, C2))
    st_y = st + other_y(st)
    st = st_y + ring_x(st_y, 1) + ring_x(st_y, 2) + ring_x(st_y, 3)
    hd, hu = (to_next(down), to_prev(up))

    wdt, wun, _ = turned([w_down, up_t], 4, after=(st_y,))
    ave, avo, low, cact, depth, cv = call(
        forward_kernel,
        [
            sds((384, 3 * C1)),
            sds((384, 3 * C1)),
            sds((128, C2)),
            sds((128, C2)),
            sds((128, 4 * C1)),
            sds((256, 3 * C2)),
        ],
        6,
        [pltpu.VMEM((640, 3 * C1), BF), pltpu.VMEM((640, 3 * C1), BF), pltpu.VMEM((256, 4 * C1), BF)],
        smem=1,
        us=7,
    )(edge, x, hd, hu, st, w_fine.reshape(3, 3 * C1, C1), w_down.reshape(4 * C1, C2))
    send, coarse = call(
        coarse_level_kernel,
        [sds((512, C1)), sds((128, C2))],
        5,
        [pltpu.VMEM((512, C1), BF)],
        us=3,
    )(cv, low, depth, w_coarse.reshape(3, 3 * C2, C2), wun)

    m0, m1, m2, m3, back = call(
        gcoarse_kernel,
        [sds((128, 960))] * 4 + [sds((128, C2), F32)],
        5,
        [pltpu.VMEM((256, 3 * C2), BF)],
        smem=1,
        us=6,
    )(me, g, hd, hu, cact, wct.reshape(3, 3 * C2, C2))
    m1, m2, m3 = (ring_z(v, n + 1) for n, v in enumerate((m1, m2, m3)))

    gres, geo, glow, up, down = call(
        gresid_kernel,
        [sds((512, C1)), sds((512, C1)), sds((128, C2)), sds((128, C1)), sds((128, C1))],
        5,
        us=3,
    )(cotk, g, back, low, wdt)
    ed, eu = (to_next(down), to_prev(up))

    gt, ct, lt = call(
        turn_grads_kernel,
        [sds((C2, 512)), sds((4, C2, 128)), sds((C2, 128))],
        3,
        smem=1,
        us=3,
        after=(m1[:8, :128] + m2[:8, :128] + m3[:8, :128],),
    )(me, geo, cotk, glow)
    kw, sw = call(
        weight_kernel,
        [sds((C1, 4224))] * 2,
        7,
        [pltpu.VMEM((C1, 2880), F32)],
        smem=1,
        us=7,
        after=(ed, eu),
    )(me, gt, ct, lt, ave, avo, coarse, depth)
    got_w = other_core(sw)
    gn, st2 = call(
        gnorm_kernel,
        [sds((512, C1), F32), sds((8, C1), F32)],
        6,
        [pltpu.VMEM((4, 384, C1), BF)],
        us=6,
        after=(sw,),
    )(x, st, geo, ed, eu, w_fine)
    pair_w, st2 = call(slab_kernel, [sds((8, 40, 4224)), sds((8, C1), F32)], 3, us=4)(
        kw.reshape(8, 40, 4224), got_w.reshape(8, 40, 4224), st2
    )
    sums_w = swap_z(pair_w.reshape(4, 80, 4224))
    kc, sc = call(
        coarse_kernel,
        [sds((16, 40, 720))] * 2,
        4,
        [pltpu.VMEM((1440, 512), BF), pltpu.VMEM((1440, C2), F32)],
        smem=1,
        us=1,
        after=(st2,),
    )(me, m0, m1, m2, m3)
    st2_y = st2 + other_y(st2)
    st2 = st2_y + ring_x(st2_y, 1) + ring_x(st2_y, 2) + ring_x(st2_y, 3)
    got_c = other_core(sc)

    pair_c = call(pair_kernel, [sds((4, 40, 720))] * 4, 2, us=1, after=(st2_y,))(kc, got_c)
    coarse_x = add(pair_c[0], *[ring_x(pair_c[n], n) for n in range(1, 4)])

    gsend, token = call(grad_latent_kernel, [sds((16, 64, C1)), sds((8, 128), F32)], 6, us=1, after=(coarse_x[0, :8, :128],))(
        x, st, gn, gres, st2, send
    )
    home = swap_wa(gsend)
    output = home[:, :32].reshape(frames, rows, cols, C1)
    grad_latent = home[:, 32:].reshape(frames, rows, cols, C1)

    packed = call(
        pack_kernel,
        [sds((2, 80, C2))] * 4,
        1,
        [
            pltpu.VMEM((80, 4224), F32),
            pltpu.VMEM((80, C2), F32),
            pltpu.VMEM((80, C2), F32),
            pltpu.VMEM((8, 80, C2), BF),
        ],
        smem=1,
        us=0,
        after=(coarse_x, token),
    )(me, sums_w)
    joined = call(join_kernel, [sds((40, 1360))] * 4, 5, us=0, after=(home[0, :8, :128],))(
        packed[0], *[ring_x(packed[n], n) for n in range(1, 4)], coarse_x
    )
    fine, down, coarse_w, up = call(
        functools.partial(finish_kernel, scale),
        [sds((9, 20, 40), F32), sds((4, 40, 40), F32), sds((9, 40, 80), F32), sds((20, 4, 80), F32)],
        4,
        [pltpu.VMEM((128, 128), F32)],
    )(joined[0], other_y(joined[2]), other_y_hi(joined[1]), other_both(joined[3]))
    fine, coarse_w = (jnp.swapaxes(v, 1, 2) for v in (fine, coarse_w))
    return output, grad_latent, fine, down, coarse_w, jnp.transpose(up, (1, 2, 0))


def solution(mesh):
    big, small = (P(None, "ha", "wa", None), P(None, "ha", "wa"))
    return jax.shard_map(
        shards,
        mesh=mesh,
        in_specs=(big, big, P(), P(), P(), P()),
        out_specs=(big, big, small, small, small, small),
        check_vma=False,
    )
```
